32 devices in a mesh: groups: 2 (over y), tensor: 4 (over x, core), dp: 4 (over z).
Axes of the slice: x: 2, y: 2, z: 4, core: 2. Of those that a mesh axis runs over, the one named last changes fastest.
Arguments:
- activations: bfloat16 [8, 512, 4096], P(('groups', 'dp'), 'tensor'), parts along dimension 0, may hold values from -6 to 6
- out_grads: bfloat16 [8, 512, 14336], P(('groups', 'dp'), None, 'tensor'), parts along dimension 0, may hold values from -1 to 1
- q_start: bfloat16 [28672, 64], P(('groups', 'tensor')), parts along dimension 0, may hold values from -0.046875 to 0.046875
Outputs:
- weight_update: bfloat16 [8192, 14336], P(('groups', 'dp'), 'tensor'), parts along dimension 0
- q_new: float32 [28672, 64], P(('groups', 'tensor')), parts along dimension 0
- new_error: bfloat16 [8, 4096, 14336], P(('groups', 'dp'), None, 'tensor'), parts along dimension 0
The draws below stay inside these ranges and needn't reach their ends.
There are 2 independent parts, one for each index of `groups`. The reference program is written for one: setup_inputs(seed, part) draws one part's arguments, and reference() takes and returns one part's arrays. A program takes and returns all parts, laid end to end along the dimension named above; each array names one. Nothing has to cross between parts.
All inputs are finite; a program needn't handle non-finite values.
Results may differ from the reference program's by a relative error of at most 0.0057.
Values may be sent and summed in bfloat16 or wider, within the bound.
A program may use at most 192 MiB of HBM per device.

```python
import jax
import jax.numpy as jnp
from jax import lax

D = 4096
FF = 14336
RANK = 64
TOK_REP = 512
N_DP = 4


def steps_of(key, dims, split, smallest, high):
    factor_of, own = 1.0, jax.random.fold_in(key, 6)
    for dim, blocks in split:
        draws = jnp.exp(jax.random.uniform(jax.random.fold_in(own, dim), (blocks,), jnp.float32, smallest / len(split), high / len(split)))
        factor_of = factor_of * jnp.repeat(draws, dims[dim] // blocks).reshape([-1 if axis == dim else 1 for axis in range(len(dims))])
    return factor_of


def gaussian(own_key, dims, scale, limit, pieces=(), dtype=jnp.bfloat16):
    entries = scale * jax.random.normal(own_key, dims, jnp.float32)
    if pieces:
        entries = entries * steps_of(own_key, dims, pieces, -0.22, 0.18)
    return jnp.clip(entries, -limit, limit).astype(dtype)


def setup_inputs(seed: int = 0, part: int = 0) -> dict:
    key_of = jax.random.split(jax.random.key(seed), 4)
    part_splits = jax.random.split(jax.random.fold_in(key_of[3], part), 4)
    return {
        "activations": gaussian(part_splits[0], (N_DP, TOK_REP, D), 1.0, 6.0, ((0, 4), (1, 4))),
        "out_grads": gaussian(part_splits[1], (N_DP, TOK_REP, FF), (TOK_REP // 16) ** -0.5, 1.0, ((0, 4), (2, 4))),
        "q_start": gaussian(part_splits[2], (FF, RANK), FF ** -0.5, 0.046875, ((0, 4),)),
    }


def reference(activations, out_grads, q_start):
    merged_list = []
    p_total = jnp.zeros((D, RANK), jnp.float32)
    for replica in range(N_DP):
        weight_grad = lax.dot_general(activations[replica].astype(jnp.float32), out_grads[replica].astype(jnp.float32), (((0,), (0,)), ((), ())), preferred_element_type=jnp.float32)
        merged = weight_grad.astype(jnp.bfloat16)
        merged_list.append(merged)
        p_total = p_total + jnp.dot(merged.astype(jnp.float32), q_start.astype(jnp.float32), preferred_element_type=jnp.float32)
    p_avg = p_total / N_DP
    gram_matrix = jnp.dot(p_avg.T, p_avg, precision=lax.Precision.HIGHEST)
    factor = jnp.linalg.cholesky(gram_matrix)
    p_orth = jax.scipy.linalg.solve_triangular(factor, p_avg.T, lower=True).T
    p_low = p_orth.astype(jnp.bfloat16)
    q_total = jnp.zeros((FF, RANK), jnp.float32)
    for merged in merged_list:
        q_total = q_total + lax.dot_general(merged.astype(jnp.float32), p_low.astype(jnp.float32), (((0,), (0,)), ((), ())), preferred_element_type=jnp.float32)
    q_new = q_total / N_DP
    decompressed = jnp.dot(p_orth, q_new.T, precision=lax.Precision.HIGHEST)
    weight_update = decompressed.astype(jnp.bfloat16)
    error_list = []
    for merged in merged_list:
        error_list.append((merged.astype(jnp.float32) - decompressed).astype(jnp.bfloat16))
    new_error = jnp.stack(error_list, axis=0)
    return (weight_update, q_new, new_error)
```

```python
import functools

import jax
import jax.numpy as jnp
from jax import lax
from jax.experimental import pallas as pl
from jax.experimental.pallas import tpu as pltpu
from jax.sharding import PartitionSpec as P

MESH = pl.DeviceIdType.MESH
HIGHEST = lax.Precision.HIGHEST
F32 = jnp.float32
BF16 = jnp.bfloat16


def dot(a, b, dims, precision=None):
    return lax.dot_general(
        a, b, (dims, ((), ())), precision=precision, preferred_element_type=F32
    )


def split(x):
    high = x.astype(BF16)
    return high, (x - high.astype(F32)).astype(BF16)


def inverse_factor(gram):
    rank = gram.shape[0]
    shape = (rank, 2 * rank)
    rows = lax.broadcasted_iota(jnp.int32, shape, 0)
    lanes = lax.broadcasted_iota(jnp.int32, shape, 1)
    eye = (lanes == rows + rank).astype(F32)
    wide = jnp.concatenate([gram, jnp.zeros_like(gram)], axis=1) + eye
    done = []
    for k in range(rank):
        top = (k // 8) * 8
        here = k - top
        column = jnp.broadcast_to(wide[:, k : k + 1], wide.shape)
        pivot_row = wide[here : here + 1, :]
        pivot = column[here : here + 1, :]
        done.append(pivot_row * lax.rsqrt(pivot))
        if k == rank - 1:
            break
        scaled = pivot_row / pivot
        below = lax.broadcasted_iota(jnp.int32, wide.shape, 0) > here
        wide = jnp.where(below, wide - column * scaled, wide)
        if here == 7:
            wide = wide[8:, :]
    return jnp.concatenate(done, axis=0)[:, rank:]


def factors_kernel(
    nt, nd, a_ref, g_ref, q_ref, acat_ref, qnew_ref,
    a_buf, g_buf, q_buf, h_loc, h_sib, h_chip, h_x, p_part, p_recv, p_all, p_t, p_neg,
    q_f32, q_part, q_recv, q_all,
    local_sems, a_sib_sems, a_x_sems, a_fwd_sems, h_sib_sems, h_x_sems,
    prs_sems, pag_sems, psib_sems, px_sems, pfwd_sems, qrs_sems, qag_sems,
):
    nx = nt // 2
    t, z = lax.axis_index("tensor"), lax.axis_index("dp")
    chip, core = t // 2, t % 2
    sibling = chip * 2 + 1 - core
    tok, depth = a_ref.shape[1], a_ref.shape[2]
    tokens = nt * tok
    rank = q_ref.shape[1]
    part = depth // nt
    chunk = part // nd
    q_rows = rank // nd
    pieces = a_x_sems.shape[2]
    piece = tok // pieces
    pending = []

    def x_peer(d):
        return lax.rem(chip + d, nx) * 2 + core

    def x_source(d):
        return lax.rem(chip + nx - d, nx) * 2 + core

    def z_peer(d):
        return lax.rem(z + d, nd)

    def z_source(d):
        return lax.rem(z + nd - d, nd)

    def send(src, dst, sems, axis, peer):
        copy = pltpu.make_async_remote_copy(
            src_ref=src, dst_ref=dst, send_sem=sems.at[0], recv_sem=sems.at[1],
            device_id={axis: peer}, device_id_type=MESH,
        )
        copy.start()
        pending.append(copy)
        return copy

    def token_rows(block, p):
        return pl.ds(pl.multiple_of(block * tok + p * piece, piece), piece)

    loads = [
        pltpu.make_async_copy(g_ref.at[0], g_buf, local_sems.at[0]),
        pltpu.make_async_copy(q_ref, q_buf, local_sems.at[1]),
        pltpu.make_async_copy(
            a_ref.at[0], a_buf.at[pl.ds(pl.multiple_of(t * tok, tok), tok)], local_sems.at[2]
        ),
    ]
    for load in loads:
        load.start()

    barrier = pltpu.get_barrier_semaphore()
    for d in range(1, nt):
        pl.semaphore_signal(
            barrier, inc=1, device_id={"tensor": lax.rem(t + d, nt)}, device_id_type=MESH
        )
    for d in range(1, nd):
        pl.semaphore_signal(barrier, inc=1, device_id={"dp": z_peer(d)}, device_id_type=MESH)
    pl.semaphore_wait(barrier, nt - 1 + nd - 1)

    a_x = {}
    for p in range(pieces):
        for d in range(1, nx):
            a_x[d, p] = send(
                a_ref.at[0, pl.ds(p * piece, piece)], a_buf.at[token_rows(t, p)],
                a_x_sems.at[d, :, p], "tensor", x_peer(d),
            )
    a_sib = send(
        a_ref.at[0], a_buf.at[pl.ds(pl.multiple_of(t * tok, tok), tok)],
        a_sib_sems, "tensor", sibling,
    )

    loads[0].wait()
    loads[1].wait()
    h_loc[...] = dot(g_buf[...], q_buf[...], ((1,), (0,))).T
    h_sib_copy = send(h_loc, h_sib, h_sib_sems, "tensor", sibling)
    h_sib_copy.wait_recv()
    h_chip[...] = h_loc[...] + h_sib[...]
    h_copies = [
        send(h_chip, h_x.at[d], h_x_sems.at[d], "tensor", x_peer(d)) for d in range(1, nx)
    ]

    a_fwd = []
    for p in range(pieces):
        for d in range(1, nx):
            a_x[d, p].wait_recv()
            rows = token_rows(x_source(d), p)
            a_fwd.append(
                send(a_buf.at[rows], a_buf.at[rows], a_fwd_sems.at[d, :, p], "tensor", sibling)
            )
    h_sum = h_chip[...]
    for d, copy in zip(range(1, nx), h_copies):
        copy.wait_recv()
        h_sum = h_sum + h_x[d]
    loads[2].wait()
    a_sib.wait_recv()
    for copy in a_fwd:
        copy.wait_recv()
    a_out = pltpu.make_async_copy(a_buf, acat_ref.at[pl.ds(0, tokens)], local_sems.at[3])
    a_out.start()

    h_both = jnp.concatenate(split(h_sum), axis=0)
    own = dot(
        h_both, a_buf[:, pl.ds(pl.multiple_of(t * part, part), part)], ((1,), (0,))
    )
    own = (own[:rank] + own[rank:]) * (1.0 / nd)
    for j in range(nd):
        p_part[j] = own[:, j * chunk : (j + 1) * chunk]
    copies = [
        send(p_part.at[z_peer(d)], p_recv.at[d], prs_sems.at[d], "dp", z_peer(d))
        for d in range(1, nd)
    ]
    total = p_part[z]
    for d, copy in zip(range(1, nd), copies):
        copy.wait_recv()
        total = total + p_recv[d]
    p_all[t, z] = total
    pag = [None] + [
        send(p_all.at[t, z], p_all.at[t, z], pag_sems.at[d], "dp", z_peer(d))
        for d in range(1, nd)
    ]
    psib, px, pfwd = [], {}, []
    for d in range(nd):
        if d:
            pag[d].wait_recv()
        block = p_all.at[t, z_source(d)]
        for e in range(1, nx):
            px[e, d] = send(block, block, px_sems.at[e, :, d], "tensor", x_peer(e))
        psib.append(send(block, block, psib_sems.at[:, d], "tensor", sibling))
    for d in range(nd):
        for e in range(1, nx):
            px[e, d].wait_recv()
            block = p_all.at[x_source(e), z_source(d)]
            pfwd.append(send(block, block, pfwd_sems.at[e, :, d], "tensor", sibling))
    for copy in psib + pfwd:
        copy.wait_recv()
    for i in range(nt):
        for j in range(nd):
            start = i * part + j * chunk
            p_t[:, start : start + chunk] = p_all[i, j]

    gram = dot(p_t[...], p_t[...], ((1,), (1,)), HIGHEST)
    inverse = inverse_factor(gram)
    p_orth = dot(inverse, p_t[...], ((1,), (0,)), HIGHEST)
    p_high, p_rest = split(p_orth)
    p_neg[0:rank] = -p_high
    p_neg[rank : 2 * rank] = -p_rest
    p_out = pltpu.make_async_copy(
        p_neg, acat_ref.at[pl.ds(tokens, 2 * rank)], local_sems.at[4]
    )
    p_out.start()

    u_both = jnp.concatenate(split(dot(p_high, a_buf[...], ((1,), (1,)))), axis=0)
    term = dot(u_both, g_buf[...], ((1,), (0,)))
    term = (term[:rank] + term[rank:]) * (1.0 / nd)
    q_f32[...] = term
    for j in range(nd):
        q_part[j] = term[j * q_rows : (j + 1) * q_rows].astype(q_part.dtype)
    copies = [
        send(q_part.at[z_peer(d)], q_recv.at[d], qrs_sems.at[d], "dp", z_peer(d))
        for d in range(1, nd)
    ]
    total = q_f32[pl.ds(pl.multiple_of(z * q_rows, q_rows), q_rows), :]
    for d, copy in zip(range(1, nd), copies):
        copy.wait_recv()
        total = total + q_recv[d].astype(F32)
    q_all[z] = total.astype(q_all.dtype)
    copies = [
        send(q_all.at[z], q_all.at[z], qag_sems.at[d], "dp", z_peer(d)) for d in range(1, nd)
    ]
    for copy in copies:
        copy.wait_recv()
    q_out = pltpu.make_async_copy(q_all, qnew_ref, local_sems.at[5])
    q_out.start()
    for copy in pending:
        copy.wait_send()
    a_out.wait()
    p_out.wait()
    q_out.wait()


def factors(nt, nd, activations, out_grads, q_start):
    tok, depth = activations.shape[1:]
    tokens, width = out_grads.shape[1:]
    rank = q_start.shape[1]
    nx = nt // 2
    pieces = 2
    part = depth // nt
    chunk = part // nd
    q_rows = rank // nd
    q_type = BF16 if q_rows % 16 == 0 else F32
    dma = pltpu.SemaphoreType.DMA
    anywhere = pl.BlockSpec(memory_space=pl.ANY)
    return pl.pallas_call(
        functools.partial(factors_kernel, nt, nd),
        out_shape=(
            jax.ShapeDtypeStruct((tokens + 2 * rank, depth), BF16),
            jax.ShapeDtypeStruct((nd, q_rows, width), q_type),
        ),
        in_specs=[anywhere] * 3,
        out_specs=(anywhere, anywhere),
        scratch_shapes=[
            pltpu.VMEM((tokens, depth), BF16),
            pltpu.VMEM((tokens, width), BF16),
            pltpu.VMEM((width, rank), BF16),
            pltpu.VMEM((rank, tokens), F32),
            pltpu.VMEM((rank, tokens), F32),
            pltpu.VMEM((rank, tokens), F32),
            pltpu.VMEM((nx, rank, tokens), F32),
            pltpu.VMEM((nd, rank, chunk), F32),
            pltpu.VMEM((nd, rank, chunk), F32),
            pltpu.VMEM((nt, nd, rank, chunk), F32),
            pltpu.VMEM((rank, depth), F32),
            pltpu.VMEM((2 * rank, depth), BF16),
            pltpu.VMEM((rank, width), F32),
            pltpu.VMEM((nd, q_rows, width), q_type),
            pltpu.VMEM((nd, q_rows, width), q_type),
            pltpu.VMEM((nd, q_rows, width), q_type),
            dma((6,)),
            dma((2,)),
            dma((nx, 2, pieces)),
            dma((nx, 2, pieces)),
            dma((2,)),
            dma((nx, 2)),
            dma((nd, 2)),
            dma((nd, 2)),
            dma((2, nd)),
            dma((nx, 2, nd)),
            dma((nx, 2, nd)),
            dma((nd, 2)),
            dma((nd, 2)),
        ],
        compiler_params=pltpu.CompilerParams(
            collective_id=0, has_side_effects=True, vmem_limit_bytes=48 * 2**20
        ),
        name="factors",
    )(activations, out_grads, q_start)


def finish_kernel(own, z_ref, acat_ref, g_ref, q_ref, wu_ref, qnew_ref, err_ref, lhs, both):
    step = pl.program_id(0)
    tokens, width = g_ref.shape[1:]
    rank = q_ref.shape[0]
    lhs[...] = acat_ref[...].T

    @pl.when(step == 0)
    def _():
        both[0:rank] = q_ref[...].astype(BF16)
        both[rank : 2 * rank] = q_ref[...].astype(BF16)
        qnew_ref[...] = q_ref[...].astype(F32).T

    columns = 512 if width % 512 == 0 else 128
    for j in range(width // columns):
        cols = slice(j * columns, (j + 1) * columns)
        minus = dot(lhs[:, tokens:], both[:, cols], ((1,), (0,)))
        err_ref[0, :, cols] = (
            dot(lhs[:, :tokens], g_ref[0, :, cols], ((1,), (0,))) + minus
        ).astype(BF16)

    @pl.when(step < own)
    def _():
        for j in range(width // columns):
            cols = slice(j * columns, (j + 1) * columns)
            minus = dot(lhs[:, tokens:], both[:, cols], ((1,), (0,)))
            wu_ref[:, cols] = (-minus).astype(BF16)


def finish(nd, acat, out_grads, q_t):
    depth = acat.shape[1]
    tokens, width = out_grads.shape[1:]
    rank = q_t.shape[0]
    rows = 256
    steps = depth // rows
    own = steps // nd

    def at(i, z):
        return lax.rem(i + z[0] * own, steps)

    z = lax.axis_index("dp").astype(jnp.int32).reshape(1)
    return pl.pallas_call(
        functools.partial(finish_kernel, own),
        out_shape=(
            jax.ShapeDtypeStruct((depth // nd, width), BF16),
            jax.ShapeDtypeStruct((width, rank), F32),
            jax.ShapeDtypeStruct((1, depth, width), BF16),
        ),
        grid_spec=pltpu.PrefetchScalarGridSpec(
            num_scalar_prefetch=1,
            grid=(steps,),
            in_specs=[
                pl.BlockSpec((acat.shape[0], rows), lambda i, z: (0, at(i, z))),
                pl.BlockSpec((1, tokens, width), lambda i, z: (0, 0, 0)),
                pl.BlockSpec((rank, width), lambda i, z: (0, 0)),
            ],
            out_specs=(
                pl.BlockSpec((rows, width), lambda i, z: (jnp.minimum(i, own - 1), 0)),
                pl.BlockSpec((width, rank), lambda i, z: (0, 0)),
                pl.BlockSpec((1, rows, width), lambda i, z: (0, at(i, z), 0)),
            ),
            scratch_shapes=[
                pltpu.VMEM((rows, acat.shape[0]), BF16),
                pltpu.VMEM((2 * rank, width), BF16),
            ],
        ),
        compiler_params=pltpu.CompilerParams(
            dimension_semantics=("arbitrary",), vmem_limit_bytes=48 * 2**20
        ),
        name="finish",
    )(z, acat, out_grads, q_t)


def per_device(nt, nd, activations, out_grads, q_start):
    acat, q_parts = factors(nt, nd, activations, out_grads, q_start)
    q_t = q_parts.reshape(q_start.shape[1], out_grads.shape[2])
    return finish(nd, acat, out_grads, q_t)


def solution(mesh):
    return jax.shard_map(
        functools.partial(per_device, mesh.shape["tensor"], mesh.shape["dp"]),
        mesh=mesh,
        in_specs=(
            P(("groups", "dp"), "tensor", None),
            P(("groups", "dp"), None, "tensor"),
            P(("groups", "tensor"), None),
        ),
        out_specs=(
            P(("groups", "dp"), "tensor"),
            P(("groups", "tensor"), None),
            P(("groups", "dp"), None, "tensor"),
        ),
        check_vma=False,
    )
```

```python
import functools

import jax
import jax.numpy as jnp
from jax import lax
from jax.experimental import pallas as pl
from jax.experimental.pallas import tpu as pltpu
from jax.sharding import PartitionSpec as P

MESH = pl.DeviceIdType.MESH
HIGHEST = lax.Precision.HIGHEST
F32 = jnp.float32
BF16 = jnp.bfloat16


def dot(a, b, dims, precision=None):
    return lax.dot_general(
        a, b, (dims, ((), ())), precision=precision, preferred_element_type=F32
    )


def split(x):
    high = x.astype(BF16)
    return high, (x - high.astype(F32)).astype(BF16)


def inverse_factor(gram):
    rank = gram.shape[0]
    shape = (rank, 2 * rank)
    rows = lax.broadcasted_iota(jnp.int32, shape, 0)
    lanes = lax.broadcasted_iota(jnp.int32, shape, 1)
    eye = (lanes == rows + rank).astype(F32)
    wide = jnp.concatenate([gram, jnp.zeros_like(gram)], axis=1) + eye
    done = []
    for k in range(rank):
        top = (k // 8) * 8
        here = k - top
        column = jnp.broadcast_to(wide[:, k : k + 1], wide.shape)
        pivot_row = wide[here : here + 1, :]
        pivot = column[here : here + 1, :]
        done.append(pivot_row * lax.rsqrt(pivot))
        if k == rank - 1:
            break
        scaled = pivot_row / pivot
        below = lax.broadcasted_iota(jnp.int32, wide.shape, 0) > here
        wide = jnp.where(below, wide - column * scaled, wide)
        if here == 7:
            wide = wide[8:, :]
    return jnp.concatenate(done, axis=0)[:, rank:]


def factors_kernel(
    nt, nd, a_ref, g_ref, q_ref, merged_ref, pneg_ref, qnew_ref,
    a_buf, g_buf, q_buf, h_loc, h_sib, h_chip, h_x, p_here, p_there, p_part, p_recv, p_all, p_t,
    p_neg, q_f32, q_part, q_recv, q_all, stage,
    local_sems, stage_sems, a_sib_sems, a_x_sems, a_fwd_sems, h_sib_sems, h_x_sems,
    ptok_sems, prs_sems, pag_sems, psib_sems, px_sems, pfwd_sems, qrs_sems, qag_sems,
):
    nx = nt // 2
    t, z = lax.axis_index("tensor"), lax.axis_index("dp")
    chip, core = t // 2, t % 2
    sibling = chip * 2 + 1 - core
    tok, depth = a_ref.shape[1], a_ref.shape[2]
    tokens = nt * tok
    rank = q_ref.shape[0]
    part = depth // nt
    chunk = part // nd
    q_rows = rank // nd
    pieces = a_x_sems.shape[2]
    early = max(1, pieces // 4)
    pair = 2 * tok
    piece = tok // pieces
    pending = []

    def x_peer(d):
        return lax.rem(chip + d, nx) * 2 + core

    def x_source(d):
        return lax.rem(chip + nx - d, nx) * 2 + core

    def z_peer(d):
        return lax.rem(z + d, nd)

    def z_source(d):
        return lax.rem(z + nd - d, nd)

    def send(src, dst, sems, axis, peer):
        copy = pltpu.make_async_remote_copy(
            src_ref=src, dst_ref=dst, send_sem=sems.at[0], recv_sem=sems.at[1],
            device_id={axis: peer}, device_id_type=MESH,
        )
        copy.start()
        pending.append(copy)
        return copy

    def token_rows(block, p):
        return pl.ds(pl.multiple_of(block * tok + p * piece, piece), piece)

    loads = [
        pltpu.make_async_copy(g_ref.at[0], g_buf, local_sems.at[0]),
        pltpu.make_async_copy(q_ref, q_buf, local_sems.at[1]),
        pltpu.make_async_copy(
            a_ref.at[0], a_buf.at[pl.ds(pl.multiple_of(t * tok, tok), tok)], local_sems.at[2]
        ),
    ]
    for load in loads:
        load.start()

    barrier = pltpu.get_barrier_semaphore()
    for d in range(1, nt):
        pl.semaphore_signal(
            barrier, inc=1, device_id={"tensor": lax.rem(t + d, nt)}, device_id_type=MESH
        )
    for d in range(1, nd):
        pl.semaphore_signal(barrier, inc=1, device_id={"dp": z_peer(d)}, device_id_type=MESH)
    pl.semaphore_wait(barrier, nt - 1 + nd - 1)

    a_x, a_fwd = {}, []

    def send_tokens(first, last):
        for p in range(first, last):
            for d in range(1, nx):
                a_x[d, p] = send(
                    a_ref.at[0, pl.ds(p * piece, piece)], a_buf.at[token_rows(t, p)],
                    a_x_sems.at[d, :, p], "tensor", x_peer(d),
                )

    def forward_tokens(first, last):
        for p in range(first, last):
            for d in range(1, nx):
                a_x[d, p].wait_recv()
                rows = token_rows(x_source(d), p)
                a_fwd.append(
                    send(
                        a_buf.at[rows], a_buf.at[rows], a_fwd_sems.at[d, :, p],
                        "tensor", sibling,
                    )
                )

    a_sib = send(
        a_ref.at[0], a_buf.at[pl.ds(pl.multiple_of(t * tok, tok), tok)],
        a_sib_sems, "tensor", sibling,
    )
    send_tokens(0, early)

    loads[0].wait()
    loads[1].wait()
    h_term = dot(q_buf[...], g_buf[...], ((1,), (1,)))
    for i in range(nx):
        h_loc[i] = h_term[:, i * pair : (i + 1) * pair]
    h_sib_copy = send(h_loc, h_sib, h_sib_sems, "tensor", sibling)
    h_sib_copy.wait_recv()
    h_chip[...] = h_loc[...] + h_sib[...]
    h_copies = [
        send(
            h_chip.at[lax.rem(chip + d, nx)], h_x.at[d], h_x_sems.at[d], "tensor", x_peer(d)
        )
        for d in range(1, nx)
    ]
    loads[2].wait()
    a_sib.wait_recv()
    h_sum = h_chip[chip]
    for d, copy in zip(range(1, nx), h_copies):
        copy.wait_recv()
        h_sum = h_sum + h_x[d]

    h_both = jnp.concatenate(split(h_sum), axis=0)
    chip_rows = pl.ds(pl.multiple_of(chip * pair, pair), pair)

    def p_rows(owner):
        columns = pl.ds(pl.multiple_of(owner * part, part), part)
        both = dot(h_both, a_buf[chip_rows, columns], ((1,), (0,)))
        return (both[:rank] + both[rank:]) * (1.0 / nd)

    ptok = []
    for d in range(1, nx):
        p_here[d] = p_rows(x_peer(d))
        ptok.append(send(p_here.at[d], p_there.at[d], ptok_sems.at[d], "tensor", x_peer(d)))
    own = p_rows(t)
    for d, copy in zip(range(1, nx), ptok):
        copy.wait_recv()
        own = own + p_there[d]
    late = max(early, pieces - pieces // 4)
    send_tokens(early, late)
    for j in range(nd):
        p_part[j] = own[:, j * chunk : (j + 1) * chunk]
    copies = [
        send(p_part.at[z_peer(d)], p_recv.at[d], prs_sems.at[d], "dp", z_peer(d))
        for d in range(1, nd)
    ]
    forward_tokens(0, early)
    total = p_part[z]
    for d, copy in zip(range(1, nd), copies):
        copy.wait_recv()
        total = total + p_recv[d]
    p_all[t, z] = total
    pag = [None] + [
        send(p_all.at[t, z], p_all.at[t, z], pag_sems.at[d], "dp", z_peer(d))
        for d in range(1, nd)
    ]
    psib, px, pfwd = [], {}, []
    for d in range(nd):
        if d:
            pag[d].wait_recv()
        block = p_all.at[t, z_source(d)]
        for e in range(1, nx):
            px[e, d] = send(block, block, px_sems.at[e, :, d], "tensor", x_peer(e))
        psib.append(send(block, block, psib_sems.at[:, d], "tensor", sibling))
    send_tokens(late, pieces)
    for d in range(nd):
        for e in range(1, nx):
            px[e, d].wait_recv()
            block = p_all.at[x_source(e), z_source(d)]
            pfwd.append(send(block, block, pfwd_sems.at[e, :, d], "tensor", sibling))
    forward_tokens(early, late)
    for copy in psib + pfwd:
        copy.wait_recv()
    for i in range(nt):
        for j in range(nd):
            start = i * part + j * chunk
            p_t[:, start : start + chunk] = p_all[i, j]

    gram = dot(p_t[...], p_t[...], ((1,), (1,)), HIGHEST)
    inverse = inverse_factor(gram)
    forward_tokens(late, pieces)
    p_orth = dot(inverse, p_t[...], ((1,), (0,)), HIGHEST)
    p_high, p_rest = split(p_orth)
    p_neg[0:rank] = -p_high
    p_neg[rank : 2 * rank] = -p_rest
    p_out = pltpu.make_async_copy(
        p_neg, pneg_ref, local_sems.at[4]
    )
    p_out.start()

    for copy in a_fwd:
        copy.wait_recv()

    rows = stage.shape[1]
    steps = depth // rows
    width = g_buf.shape[1]
    columns = 512 if width % 512 == 0 else 128

    def write(slot, row):
        return pltpu.make_async_copy(
            stage.at[slot], merged_ref.at[pl.ds(row, rows)], stage_sems.at[slot]
        )

    def merge(i, _):
        slot = lax.rem(i, 2)
        row = pl.multiple_of(i * rows, rows)

        @pl.when(i >= 2)
        def _():
            write(slot, row).wait()

        lhs = a_buf[:, pl.ds(row, rows)].T
        for j in range(width // columns):
            cols = slice(j * columns, (j + 1) * columns)
            stage[slot, :, cols] = dot(lhs, g_buf[:, cols], ((1,), (0,))).astype(BF16)
        write(slot, row).start()
        return 0

    u_both = jnp.concatenate(split(dot(p_high, a_buf[...], ((1,), (1,)))), axis=0)
    term = dot(u_both, g_buf[...], ((1,), (0,)))
    term = (term[:rank] + term[rank:]) * (1.0 / nd)
    q_f32[...] = term
    for j in range(nd):
        q_part[j] = term[j * q_rows : (j + 1) * q_rows].astype(q_part.dtype)
    copies = [
        send(q_part.at[z_peer(d)], q_recv.at[d], qrs_sems.at[d], "dp", z_peer(d))
        for d in range(1, nd)
    ]
    lax.fori_loop(0, steps // 2, merge, 0)
    total = q_f32[pl.ds(pl.multiple_of(z * q_rows, q_rows), q_rows), :]
    for d, copy in zip(range(1, nd), copies):
        copy.wait_recv()
        total = total + q_recv[d].astype(F32)
    q_all[z] = total.astype(q_all.dtype)
    copies = [
        send(q_all.at[z], q_all.at[z], qag_sems.at[d], "dp", z_peer(d)) for d in range(1, nd)
    ]
    lax.fori_loop(steps // 2, steps, merge, 0)
    for copy in copies:
        copy.wait_recv()
    q_out = pltpu.make_async_copy(q_all, qnew_ref, local_sems.at[5])
    q_out.start()
    for copy in pending:
        copy.wait_send()
    for slot in range(2):
        write(slot, 0).wait()
    p_out.wait()
    q_out.wait()


def factors(nt, nd, activations, out_grads, q_t):
    tok, depth = activations.shape[1:]
    tokens, width = out_grads.shape[1:]
    rank = q_t.shape[0]
    nx = nt // 2
    pair = 2 * tok
    pieces = min(4, tok // 16)
    part = depth // nt
    chunk = part // nd
    q_rows = rank // nd
    q_type = BF16 if q_rows % 16 == 0 else F32
    dma = pltpu.SemaphoreType.DMA
    anywhere = pl.BlockSpec(memory_space=pl.ANY)
    return pl.pallas_call(
        functools.partial(factors_kernel, nt, nd),
        out_shape=(
            jax.ShapeDtypeStruct((depth, width), BF16),
            jax.ShapeDtypeStruct((2 * rank, depth), BF16),
            jax.ShapeDtypeStruct((nd, q_rows, width), q_type),
        ),
        in_specs=[anywhere] * 3,
        out_specs=(anywhere, anywhere, anywhere),
        scratch_shapes=[
            pltpu.VMEM((tokens, depth), BF16),
            pltpu.VMEM((tokens, width), BF16),
            pltpu.VMEM((rank, width), BF16),
            pltpu.VMEM((nx, rank, pair), F32),
            pltpu.VMEM((nx, rank, pair), F32),
            pltpu.VMEM((nx, rank, pair), F32),
            pltpu.VMEM((nx, rank, pair), F32),
            pltpu.VMEM((nx, rank, part), F32),
            pltpu.VMEM((nx, rank, part), F32),
            pltpu.VMEM((nd, rank, chunk), F32),
            pltpu.VMEM((nd, rank, chunk), F32),
            pltpu.VMEM((nt, nd, rank, chunk), F32),
            pltpu.VMEM((rank, depth), F32),
            pltpu.VMEM((2 * rank, depth), BF16),
            pltpu.VMEM((rank, width), F32),
            pltpu.VMEM((nd, q_rows, width), q_type),
            pltpu.VMEM((nd, q_rows, width), q_type),
            pltpu.VMEM((nd, q_rows, width), q_type),
            pltpu.VMEM((2, 512, width), BF16),
            dma((6,)),
            dma((2,)),
            dma((2,)),
            dma((nx, 2, pieces)),
            dma((nx, 2, pieces)),
            dma((2,)),
            dma((nx, 2)),
            dma((nx, 2)),
            dma((nd, 2)),
            dma((nd, 2)),
            dma((2, nd)),
            dma((nx, 2, nd)),
            dma((nx, 2, nd)),
            dma((nd, 2)),
            dma((nd, 2)),
        ],
        compiler_params=pltpu.CompilerParams(
            collective_id=0, has_side_effects=True, vmem_limit_bytes=61 * 2**20
        ),
        name="factors",
    )(activations, out_grads, q_t)


def finish_kernel(own, z_ref, merged_ref, pneg_ref, q_ref, wu_ref, qnew_ref, err_ref, lhs, both):
    step = pl.program_id(0)
    width = merged_ref.shape[1]
    rank = q_ref.shape[0]
    lhs[...] = pneg_ref[...].T

    @pl.when(step == 0)
    def _():
        both[0:rank] = q_ref[...].astype(BF16)
        both[rank : 2 * rank] = q_ref[...].astype(BF16)
        qnew_ref[...] = q_ref[...].astype(F32)

    columns = 512 if width % 512 == 0 else 128

    def tiles(update):
        for j in range(width // columns):
            cols = slice(j * columns, (j + 1) * columns)
            minus = dot(lhs[...], both[:, cols], ((1,), (0,)))
            err_ref[0, :, cols] = (merged_ref[:, cols].astype(F32) + minus).astype(BF16)
            if update:
                wu_ref[:, cols] = (-minus).astype(BF16)

    pl.when(step < own)(lambda: tiles(True))
    pl.when(step >= own)(lambda: tiles(False))


def finish(nd, merged, p_neg, q_t):
    depth, width = merged.shape
    rank = q_t.shape[0]
    rows = 256
    steps = depth // rows
    own = steps // nd

    def at(i, z):
        return lax.rem(i + z[0] * own, steps)

    z = lax.axis_index("dp").astype(jnp.int32).reshape(1)
    return pl.pallas_call(
        functools.partial(finish_kernel, own),
        out_shape=(
            jax.ShapeDtypeStruct((depth // nd, width), BF16),
            jax.ShapeDtypeStruct((rank, width), F32),
            jax.ShapeDtypeStruct((1, depth, width), BF16),
        ),
        grid_spec=pltpu.PrefetchScalarGridSpec(
            num_scalar_prefetch=1,
            grid=(steps,),
            in_specs=[
                pl.BlockSpec((rows, width), lambda i, z: (at(i, z), 0)),
                pl.BlockSpec((2 * rank, rows), lambda i, z: (0, at(i, z))),
                pl.BlockSpec((rank, width), lambda i, z: (0, 0)),
            ],
            out_specs=(
                pl.BlockSpec((rows, width), lambda i, z: (jnp.minimum(i, own - 1), 0)),
                pl.BlockSpec((rank, width), lambda i, z: (0, 0)),
                pl.BlockSpec((1, rows, width), lambda i, z: (0, at(i, z), 0)),
            ),
            scratch_shapes=[
                pltpu.VMEM((rows, 2 * rank), BF16),
                pltpu.VMEM((2 * rank, width), BF16),
            ],
        ),
        compiler_params=pltpu.CompilerParams(
            dimension_semantics=("arbitrary",), vmem_limit_bytes=30 * 2**20
        ),
        name="finish",
    )(z, merged, p_neg, q_t)


def per_device(nt, nd, activations, out_grads, q_start):
    merged, p_neg, q_parts = factors(nt, nd, activations, out_grads, q_start.T)
    q_t = q_parts.reshape(q_start.shape[1], out_grads.shape[2])
    weight_update, q_new, new_error = finish(nd, merged, p_neg, q_t)
    return weight_update, q_new.T, new_error


def solution(mesh):
    return jax.shard_map(
        functools.partial(per_device, mesh.shape["tensor"], mesh.shape["dp"]),
        mesh=mesh,
        in_specs=(
            P(("groups", "dp"), "tensor", None),
            P(("groups", "dp"), None, "tensor"),
            P(("groups", "tensor"), None),
        ),
        out_specs=(
            P(("groups", "dp"), "tensor"),
            P(("groups", "tensor"), None),
            P(("groups", "dp"), None, "tensor"),
        ),
        check_vma=False,
    )
```

```python
import functools

import jax
import jax.numpy as jnp
from jax import lax
from jax.experimental import pallas as pl
from jax.experimental.pallas import tpu as pltpu
from jax.sharding import PartitionSpec as P

MESH = pl.DeviceIdType.MESH
HIGHEST = lax.Precision.HIGHEST
F32 = jnp.float32
BF16 = jnp.bfloat16


def dot(a, b, dims, precision=None):
    return lax.dot_general(
        a, b, (dims, ((), ())), precision=precision, preferred_element_type=F32
    )


def split(x):
    high = x.astype(BF16)
    return high, (x - high.astype(F32)).astype(BF16)


def inverse_factor(gram):
    rank = gram.shape[0]
    shape = (rank, 2 * rank)
    rows = lax.broadcasted_iota(jnp.int32, shape, 0)
    lanes = lax.broadcasted_iota(jnp.int32, shape, 1)
    eye = (lanes == rows + rank).astype(F32)
    wide = jnp.concatenate([gram, jnp.zeros_like(gram)], axis=1) + eye
    done = []
    group = 8
    for top in range(0, rank, group):
        columns = [
            jnp.broadcast_to(wide[:, top + i : top + i + 1], wide.shape) for i in range(group)
        ]
        for i in range(group):
            pivot_row = wide[i : i + 1, :]
            pivot = columns[i][i : i + 1, :]
            inverse = 1.0 / pivot
            done.append(pivot_row * lax.rsqrt(pivot))
            wide = wide - columns[i] * (pivot_row * inverse)
            for j in range(i + 1, group):
                columns[j] = columns[j] - columns[i] * (columns[j][i : i + 1, :] * inverse)
        wide = wide[group:, :]
    return jnp.concatenate(done, axis=0)[:, rank:]


def factors_kernel(
    nt, nd, a_ref, g_ref, q_ref, merged_ref, pneg_ref, qnew_ref,
    a_buf, g_buf, q_buf, h_loc, h_sib, h_chip, h_x, p_here, p_there, p_part, p_recv, p_all, p_t,
    p_neg, q_f32, q_part, q_recv, q_all, stage,
    local_sems, stage_sems, a_sib_sems, a_x_sems, a_fwd_sems, h_sib_sems, h_x_sems,
    ptok_sems, prs_sems, pag_sems, psib_sems, px_sems, pfwd_sems, qrs_sems, qag_sems,
):
    nx = nt // 2
    t, z = lax.axis_index("tensor"), lax.axis_index("dp")
    chip, core = t // 2, t % 2
    sibling = chip * 2 + 1 - core
    tok, depth = a_ref.shape[1], a_ref.shape[2]
    tokens = nt * tok
    rank = q_ref.shape[0]
    part = depth // nt
    chunk = part // nd
    q_rows = rank // nd
    pieces = a_x_sems.shape[2]
    early = max(1, pieces // 4)
    pair = 2 * tok
    piece = tok // pieces
    pending = []

    def x_peer(d):
        return lax.rem(chip + d, nx) * 2 + core

    def x_source(d):
        return lax.rem(chip + nx - d, nx) * 2 + core

    def z_peer(d):
        return lax.rem(z + d, nd)

    def z_source(d):
        return lax.rem(z + nd - d, nd)

    def send(src, dst, sems, axis, peer):
        copy = pltpu.make_async_remote_copy(
            src_ref=src, dst_ref=dst, send_sem=sems.at[0], recv_sem=sems.at[1],
            device_id={axis: peer}, device_id_type=MESH,
        )
        copy.start()
        pending.append(copy)
        return copy

    def token_rows(block, p):
        return pl.ds(pl.multiple_of(block * tok + p * piece, piece), piece)

    loads = [
        pltpu.make_async_copy(g_ref.at[0], g_buf, local_sems.at[0]),
        pltpu.make_async_copy(q_ref, q_buf, local_sems.at[1]),
        pltpu.make_async_copy(
            a_ref.at[0], a_buf.at[pl.ds(pl.multiple_of(t * tok, tok), tok)], local_sems.at[2]
        ),
    ]
    for load in loads:
        load.start()

    barrier = pltpu.get_barrier_semaphore()
    for d in range(1, nt):
        pl.semaphore_signal(
            barrier, inc=1, device_id={"tensor": lax.rem(t + d, nt)}, device_id_type=MESH
        )
    for d in range(1, nd):
        pl.semaphore_signal(barrier, inc=1, device_id={"dp": z_peer(d)}, device_id_type=MESH)
    pl.semaphore_wait(barrier, nt - 1 + nd - 1)

    a_x, a_fwd = {}, []

    def send_tokens(first, last):
        for p in range(first, last):
            for d in range(1, nx):
                a_x[d, p] = send(
                    a_ref.at[0, pl.ds(p * piece, piece)], a_buf.at[token_rows(t, p)],
                    a_x_sems.at[d, :, p], "tensor", x_peer(d),
                )

    def forward_tokens(first, last):
        for p in range(first, last):
            for d in range(1, nx):
                a_x[d, p].wait_recv()
                rows = token_rows(x_source(d), p)
                a_fwd.append(
                    send(
                        a_buf.at[rows], a_buf.at[rows], a_fwd_sems.at[d, :, p],
                        "tensor", sibling,
                    )
                )

    a_sib = send(
        a_ref.at[0], a_buf.at[pl.ds(pl.multiple_of(t * tok, tok), tok)],
        a_sib_sems, "tensor", sibling,
    )
    send_tokens(0, early)

    loads[0].wait()
    loads[1].wait()
    h_term = dot(q_buf[...], g_buf[...], ((1,), (1,)))
    for i in range(nx):
        h_loc[i] = h_term[:, i * pair : (i + 1) * pair]
    h_sib_copy = send(h_loc, h_sib, h_sib_sems, "tensor", sibling)
    h_sib_copy.wait_recv()
    h_chip[...] = h_loc[...] + h_sib[...]
    h_copies = [
        send(
            h_chip.at[lax.rem(chip + d, nx)], h_x.at[d], h_x_sems.at[d], "tensor", x_peer(d)
        )
        for d in range(1, nx)
    ]
    loads[2].wait()
    a_sib.wait_recv()
    h_sum = h_chip[chip]
    for d, copy in zip(range(1, nx), h_copies):
        copy.wait_recv()
        h_sum = h_sum + h_x[d]

    h_both = jnp.concatenate(split(h_sum), axis=0)
    chip_rows = pl.ds(pl.multiple_of(chip * pair, pair), pair)

    def p_rows(owner):
        columns = pl.ds(pl.multiple_of(owner * part, part), part)
        both = dot(h_both, a_buf[chip_rows, columns], ((1,), (0,)))
        return (both[:rank] + both[rank:]) * (1.0 / nd)

    ptok = []
    for d in range(1, nx):
        p_here[d] = p_rows(x_peer(d))
        ptok.append(send(p_here.at[d], p_there.at[d], ptok_sems.at[d], "tensor", x_peer(d)))
    own = p_rows(t)
    for d, copy in zip(range(1, nx), ptok):
        copy.wait_recv()
        own = own + p_there[d]
    late = max(early, pieces - pieces // 4)
    send_tokens(early, late)
    for j in range(nd):
        p_part[j] = own[:, j * chunk : (j + 1) * chunk]
    copies = [
        send(p_part.at[z_peer(d)], p_recv.at[d], prs_sems.at[d], "dp", z_peer(d))
        for d in range(1, nd)
    ]
    forward_tokens(0, early)
    total = p_part[z]
    for d, copy in zip(range(1, nd), copies):
        copy.wait_recv()
        total = total + p_recv[d]
    p_all[t, z] = total
    pag = [None] + [
        send(p_all.at[t, z], p_all.at[t, z], pag_sems.at[d], "dp", z_peer(d))
        for d in range(1, nd)
    ]
    psib, px, pfwd = [], {}, []
    for d in range(nd):
        if d:
            pag[d].wait_recv()
        block = p_all.at[t, z_source(d)]
        for e in range(1, nx):
            px[e, d] = send(block, block, px_sems.at[e, :, d], "tensor", x_peer(e))
        psib.append(send(block, block, psib_sems.at[:, d], "tensor", sibling))
    send_tokens(late, pieces)
    for d in range(nd):
        for e in range(1, nx):
            px[e, d].wait_recv()
            block = p_all.at[x_source(e), z_source(d)]
            pfwd.append(send(block, block, pfwd_sems.at[e, :, d], "tensor", sibling))
    forward_tokens(early, late)
    for copy in psib + pfwd:
        copy.wait_recv()
    for i in range(nt):
        for j in range(nd):
            start = i * part + j * chunk
            p_t[:, start : start + chunk] = p_all[i, j]

    gram = dot(p_t[...], p_t[...], ((1,), (1,)), HIGHEST)
    inverse = inverse_factor(gram)
    forward_tokens(late, pieces)
    p_orth = dot(inverse, p_t[...], ((1,), (0,)), HIGHEST)
    p_high, p_rest = split(p_orth)
    p_neg[0:rank] = -p_high
    p_neg[rank : 2 * rank] = -p_rest
    p_out = pltpu.make_async_copy(
        p_neg, pneg_ref, local_sems.at[4]
    )
    p_out.start()

    for copy in a_fwd:
        copy.wait_recv()

    rows = stage.shape[1]
    steps = depth // rows
    width = g_buf.shape[1]
    columns = 512 if width % 512 == 0 else 128

    def write(slot, row):
        return pltpu.make_async_copy(
            stage.at[slot], merged_ref.at[pl.ds(row, rows)], stage_sems.at[slot]
        )

    def merge(i, _):
        slot = lax.rem(i, 2)
        row = pl.multiple_of(i * rows, rows)

        @pl.when(i >= 2)
        def _():
            write(slot, row).wait()

        lhs = a_buf[:, pl.ds(row, rows)].T
        for j in range(width // columns):
            cols = slice(j * columns, (j + 1) * columns)
            stage[slot, :, cols] = dot(lhs, g_buf[:, cols], ((1,), (0,))).astype(BF16)
        write(slot, row).start()
        return 0

    u_both = jnp.concatenate(split(dot(p_high, a_buf[...], ((1,), (1,)))), axis=0)
    term = dot(u_both, g_buf[...], ((1,), (0,)))
    term = (term[:rank] + term[rank:]) * (1.0 / nd)
    q_f32[...] = term
    for j in range(nd):
        q_part[j] = term[j * q_rows : (j + 1) * q_rows].astype(q_part.dtype)
    copies = [
        send(q_part.at[z_peer(d)], q_recv.at[d], qrs_sems.at[d], "dp", z_peer(d))
        for d in range(1, nd)
    ]
    lax.fori_loop(0, steps // 2, merge, 0)
    total = q_f32[pl.ds(pl.multiple_of(z * q_rows, q_rows), q_rows), :]
    for d, copy in zip(range(1, nd), copies):
        copy.wait_recv()
        total = total + q_recv[d].astype(F32)
    q_all[z] = total.astype(q_all.dtype)
    copies = [
        send(q_all.at[z], q_all.at[z], qag_sems.at[d], "dp", z_peer(d)) for d in range(1, nd)
    ]
    lax.fori_loop(steps // 2, steps, merge, 0)
    for copy in copies:
        copy.wait_recv()
    q_out = pltpu.make_async_copy(q_all, qnew_ref, local_sems.at[5])
    q_out.start()
    for copy in pending:
        copy.wait_send()
    for slot in range(2):
        write(slot, 0).wait()
    p_out.wait()
    q_out.wait()


def factors(nt, nd, activations, out_grads, q_t):
    tok, depth = activations.shape[1:]
    tokens, width = out_grads.shape[1:]
    rank = q_t.shape[0]
    nx = nt // 2
    pair = 2 * tok
    pieces = min(4, tok // 16)
    part = depth // nt
    chunk = part // nd
    q_rows = rank // nd
    q_type = BF16 if q_rows % 16 == 0 else F32
    dma = pltpu.SemaphoreType.DMA
    anywhere = pl.BlockSpec(memory_space=pl.ANY)
    return pl.pallas_call(
        functools.partial(factors_kernel, nt, nd),
        out_shape=(
            pltpu.VMEM((depth, width), BF16),
            pltpu.VMEM((2 * rank, depth), BF16),
            pltpu.VMEM((nd, q_rows, width), q_type),
        ),
        in_specs=[anywhere] * 3,
        out_specs=(anywhere, anywhere, anywhere),
        scratch_shapes=[
            pltpu.VMEM((tokens, depth), BF16),
            pltpu.VMEM((tokens, width), BF16),
            pltpu.VMEM((rank, width), BF16),
            pltpu.VMEM((nx, rank, pair), F32),
            pltpu.VMEM((nx, rank, pair), F32),
            pltpu.VMEM((nx, rank, pair), F32),
            pltpu.VMEM((nx, rank, pair), F32),
            pltpu.VMEM((nx, rank, part), F32),
            pltpu.VMEM((nx, rank, part), F32),
            pltpu.VMEM((nd, rank, chunk), F32),
            pltpu.VMEM((nd, rank, chunk), F32),
            pltpu.VMEM((nt, nd, rank, chunk), F32),
            pltpu.VMEM((rank, depth), F32),
            pltpu.VMEM((2 * rank, depth), BF16),
            pltpu.VMEM((rank, width), F32),
            pltpu.VMEM((nd, q_rows, width), q_type),
            pltpu.VMEM((nd, q_rows, width), q_type),
            pltpu.VMEM((nd, q_rows, width), q_type),
            pltpu.VMEM((2, 512, width), BF16),
            dma((6,)),
            dma((2,)),
            dma((2,)),
            dma((nx, 2, pieces)),
            dma((nx, 2, pieces)),
            dma((2,)),
            dma((nx, 2)),
            dma((nx, 2)),
            dma((nd, 2)),
            dma((nd, 2)),
            dma((2, nd)),
            dma((nx, 2, nd)),
            dma((nx, 2, nd)),
            dma((nd, 2)),
            dma((nd, 2)),
        ],
        compiler_params=pltpu.CompilerParams(
            collective_id=0, has_side_effects=True, vmem_limit_bytes=34 * 2**20
        ),
        name="factors",
    )(activations, out_grads, q_t)


def finish_kernel(own, z_ref, merged_ref, pneg_ref, q_ref, wu_ref, qnew_ref, err_ref, lhs, both):
    step = pl.program_id(0)
    width = merged_ref.shape[1]
    rank = q_ref.shape[0]
    lhs[...] = pneg_ref[...].T

    @pl.when(step == 0)
    def _():
        both[0:rank] = q_ref[...].astype(BF16)
        both[rank : 2 * rank] = q_ref[...].astype(BF16)
        qnew_ref[...] = q_ref[...].astype(F32)

    columns = 512 if width % 512 == 0 else 128

    def tiles(update):
        for j in range(width // columns):
            cols = slice(j * columns, (j + 1) * columns)
            minus = dot(lhs[...], both[:, cols], ((1,), (0,)))
            err_ref[0, :, cols] = (merged_ref[:, cols].astype(F32) + minus).astype(BF16)
            if update:
                wu_ref[:, cols] = (-minus).astype(BF16)

    pl.when(step < own)(lambda: tiles(True))
    pl.when(step >= own)(lambda: tiles(False))


def finish(nd, merged, p_neg, q_t):
    depth, width = merged.shape
    rank = q_t.shape[0]
    rows = 256
    steps = depth // rows
    own = steps // nd

    def at(i, z):
        return lax.rem(i + z[0] * own, steps)

    z = lax.axis_index("dp").astype(jnp.int32).reshape(1)
    return pl.pallas_call(
        functools.partial(finish_kernel, own),
        out_shape=(
            jax.ShapeDtypeStruct((depth // nd, width), BF16),
            jax.ShapeDtypeStruct((rank, width), F32),
            jax.ShapeDtypeStruct((1, depth, width), BF16),
        ),
        grid_spec=pltpu.PrefetchScalarGridSpec(
            num_scalar_prefetch=1,
            grid=(steps,),
            in_specs=[
                pl.BlockSpec((rows, width), lambda i, z: (at(i, z), 0)),
                pl.BlockSpec((2 * rank, rows), lambda i, z: (0, at(i, z))),
                pl.BlockSpec((rank, width), lambda i, z: (0, 0)),
            ],
            out_specs=(
                pl.BlockSpec((rows, width), lambda i, z: (jnp.minimum(i, own - 1), 0)),
                pl.BlockSpec((rank, width), lambda i, z: (0, 0)),
                pl.BlockSpec((1, rows, width), lambda i, z: (0, at(i, z), 0)),
            ),
            scratch_shapes=[
                pltpu.VMEM((rows, 2 * rank), BF16),
                pltpu.VMEM((2 * rank, width), BF16),
            ],
        ),
        compiler_params=pltpu.CompilerParams(
            dimension_semantics=("arbitrary",), vmem_limit_bytes=34 * 2**20
        ),
        name="finish",
    )(z, merged, p_neg, q_t)


def per_device(nt, nd, activations, out_grads, q_start):
    merged, p_neg, q_parts = factors(nt, nd, activations, out_grads, q_start.T)
    q_t = q_parts.reshape(q_start.shape[1], out_grads.shape[2])
    merged, p_neg, q_t = (
        pltpu.with_memory_space_constraint(x, pltpu.VMEM) for x in (merged, p_neg, q_t)
    )
    weight_update, q_new, new_error = finish(nd, merged, p_neg, q_t)
    return weight_update, q_new.T, new_error


def solution(mesh):
    return jax.shard_map(
        functools.partial(per_device, mesh.shape["tensor"], mesh.shape["dp"]),
        mesh=mesh,
        in_specs=(
            P(("groups", "dp"), "tensor", None),
            P(("groups", "dp"), None, "tensor"),
            P(("groups", "tensor"), None),
        ),
        out_specs=(
            P(("groups", "dp"), "tensor"),
            P(("groups", "tensor"), None),
            P(("groups", "dp"), None, "tensor"),
        ),
        check_vma=False,
    )
```

```python
import functools

import jax
import jax.numpy as jnp
from jax import lax
from jax.experimental import pallas as pl
from jax.experimental.pallas import tpu as pltpu
from jax.sharding import PartitionSpec as P

MESH = pl.DeviceIdType.MESH
HIGHEST = lax.Precision.HIGHEST
F32 = jnp.float32
BF16 = jnp.bfloat16


def dot(a, b, dims, precision=None):
    return lax.dot_general(
        a, b, (dims, ((), ())), precision=precision, preferred_element_type=F32
    )


def split(x):
    high = x.astype(BF16)
    return high, (x - high.astype(F32)).astype(BF16)


def inverse_factor(gram):
    rank = gram.shape[0]
    shape = (rank, 2 * rank)
    rows = lax.broadcasted_iota(jnp.int32, shape, 0)
    lanes = lax.broadcasted_iota(jnp.int32, shape, 1)
    eye = (lanes == rows + rank).astype(F32)
    wide = jnp.concatenate([gram, jnp.zeros_like(gram)], axis=1) + eye
    done = []
    group = 8
    for top in range(0, rank, group):
        columns = [
            jnp.broadcast_to(wide[:, top + i : top + i + 1], wide.shape) for i in range(group)
        ]
        for i in range(group):
            pivot_row = wide[i : i + 1, :]
            pivot = columns[i][i : i + 1, :]
            inverse = 1.0 / pivot
            done.append(pivot_row * lax.rsqrt(pivot))
            wide = wide - columns[i] * (pivot_row * inverse)
            for j in range(i + 1, group):
                columns[j] = columns[j] - columns[i] * (columns[j][i : i + 1, :] * inverse)
        wide = wide[group:, :]
    return jnp.concatenate(done, axis=0)[:, rank:]


def factors_kernel(
    nt, nd, a_ref, g_ref, q_ref, merged_ref, pneg_ref, qnew_ref,
    a_buf, g_buf, q_buf, h_loc, h_sib, h_chip, h_x, p_here, p_there, p_part, p_recv, p_all, p_t,
    p_neg, q_f32, q_part, q_recv, q_all, stage,
    local_sems, stage_sems, a_sib_sems, a_x_sems, a_fwd_sems, h_sib_sems, h_x_sems,
    ptok_sems, prs_sems, pag_sems, psib_sems, px_sems, pfwd_sems, qrs_sems, qag_sems,
):
    nx = nt // 2
    t, z = lax.axis_index("tensor"), lax.axis_index("dp")
    chip, core = t // 2, t % 2
    sibling = chip * 2 + 1 - core
    tok, depth = a_ref.shape[1], a_ref.shape[2]
    tokens = nt * tok
    rank = q_ref.shape[0]
    part = depth // nt
    chunk = part // nd
    q_rows = rank // nd
    pieces = a_x_sems.shape[2]
    early = max(1, pieces // 4)
    pair = 2 * tok
    piece = tok // pieces
    pending = []

    def x_peer(d):
        return lax.rem(chip + d, nx) * 2 + core

    def x_source(d):
        return lax.rem(chip + nx - d, nx) * 2 + core

    def z_peer(d):
        return lax.rem(z + d, nd)

    def z_source(d):
        return lax.rem(z + nd - d, nd)

    def send(src, dst, sems, axis, peer):
        copy = pltpu.make_async_remote_copy(
            src_ref=src, dst_ref=dst, send_sem=sems.at[0], recv_sem=sems.at[1],
            device_id={axis: peer}, device_id_type=MESH,
        )
        copy.start()
        pending.append(copy)
        return copy

    def token_rows(block, p):
        return pl.ds(pl.multiple_of(block * tok + p * piece, piece), piece)

    loads = [
        pltpu.make_async_copy(g_ref.at[0], g_buf, local_sems.at[0]),
        pltpu.make_async_copy(q_ref, q_buf, local_sems.at[1]),
        pltpu.make_async_copy(
            a_ref.at[0], a_buf.at[pl.ds(pl.multiple_of(t * tok, tok), tok)], local_sems.at[2]
        ),
    ]
    for load in loads:
        load.start()

    barrier = pltpu.get_barrier_semaphore()
    for d in range(1, nt):
        pl.semaphore_signal(
            barrier, inc=1, device_id={"tensor": lax.rem(t + d, nt)}, device_id_type=MESH
        )
    for d in range(1, nd):
        pl.semaphore_signal(barrier, inc=1, device_id={"dp": z_peer(d)}, device_id_type=MESH)
    pl.semaphore_wait(barrier, nt - 1 + nd - 1)

    a_x, a_fwd = {}, []

    def send_tokens(first, last):
        for p in range(first, last):
            for d in range(1, nx):
                a_x[d, p] = send(
                    a_ref.at[0, pl.ds(p * piece, piece)], a_buf.at[token_rows(t, p)],
                    a_x_sems.at[d, :, p], "tensor", x_peer(d),
                )

    def forward_tokens(first, last):
        for p in range(first, last):
            for d in range(1, nx):
                a_x[d, p].wait_recv()
                rows = token_rows(x_source(d), p)
                a_fwd.append(
                    send(
                        a_buf.at[rows], a_buf.at[rows], a_fwd_sems.at[d, :, p],
                        "tensor", sibling,
                    )
                )

    a_sib = send(
        a_ref.at[0], a_buf.at[pl.ds(pl.multiple_of(t * tok, tok), tok)],
        a_sib_sems, "tensor", sibling,
    )
    send_tokens(0, early)

    loads[0].wait()
    loads[1].wait()
    h_term = dot(q_buf[...], g_buf[...], ((1,), (1,)))
    for i in range(nx):
        h_loc[i] = h_term[:, i * pair : (i + 1) * pair]
    h_sib_copy = send(h_loc, h_sib, h_sib_sems, "tensor", sibling)
    h_sib_copy.wait_recv()
    h_chip[...] = h_loc[...] + h_sib[...]
    h_copies = [
        send(
            h_chip.at[lax.rem(chip + d, nx)], h_x.at[d], h_x_sems.at[d], "tensor", x_peer(d)
        )
        for d in range(1, nx)
    ]
    loads[2].wait()
    a_sib.wait_recv()
    h_sum = h_chip[chip]
    for d, copy in zip(range(1, nx), h_copies):
        copy.wait_recv()
        h_sum = h_sum + h_x[d]

    h_both = jnp.concatenate(split(h_sum), axis=0)
    chip_rows = pl.ds(pl.multiple_of(chip * pair, pair), pair)

    def p_rows(owner):
        columns = pl.ds(pl.multiple_of(owner * part, part), part)
        both = dot(h_both, a_buf[chip_rows, columns], ((1,), (0,)))
        return (both[:rank] + both[rank:]) * (1.0 / nd)

    ptok = []
    for d in range(1, nx):
        p_here[d] = p_rows(x_peer(d))
        ptok.append(send(p_here.at[d], p_there.at[d], ptok_sems.at[d], "tensor", x_peer(d)))
    own = p_rows(t)
    for d, copy in zip(range(1, nx), ptok):
        copy.wait_recv()
        own = own + p_there[d]
    late = early + (pieces - early) // 3
    send_tokens(early, late)
    for j in range(nd):
        p_part[j] = own[:, j * chunk : (j + 1) * chunk]
    copies = [
        send(p_part.at[z_peer(d)], p_recv.at[d], prs_sems.at[d], "dp", z_peer(d))
        for d in range(1, nd)
    ]
    forward_tokens(0, early)
    total = p_part[z]
    for d, copy in zip(range(1, nd), copies):
        copy.wait_recv()
        total = total + p_recv[d]
    p_all[t, z] = total
    pag = [None] + [
        send(p_all.at[t, z], p_all.at[t, z], pag_sems.at[d], "dp", z_peer(d))
        for d in range(1, nd)
    ]
    psib, px, pfwd = [], {}, []
    for d in range(nd):
        if d:
            pag[d].wait_recv()
        block = p_all.at[t, z_source(d)]
        for e in range(1, nx):
            px[e, d] = send(block, block, px_sems.at[e, :, d], "tensor", x_peer(e))
        psib.append(send(block, block, psib_sems.at[:, d], "tensor", sibling))
    send_tokens(late, pieces)
    for d in range(nd):
        for e in range(1, nx):
            px[e, d].wait_recv()
            block = p_all.at[x_source(e), z_source(d)]
            pfwd.append(send(block, block, pfwd_sems.at[e, :, d], "tensor", sibling))
    forward_tokens(early, late)
    for copy in psib + pfwd:
        copy.wait_recv()
    for i in range(nt):
        for j in range(nd):
            start = i * part + j * chunk
            p_t[:, start : start + chunk] = p_all[i, j]

    gram = dot(p_t[...], p_t[...], ((1,), (1,)), HIGHEST)
    inverse = inverse_factor(gram)
    forward_tokens(late, pieces)
    p_orth = dot(inverse, p_t[...], ((1,), (0,)), HIGHEST)
    p_high, p_rest = split(p_orth)
    p_neg[0:rank] = -p_high
    p_neg[rank : 2 * rank] = -p_rest
    p_out = pltpu.make_async_copy(
        p_neg, pneg_ref, local_sems.at[4]
    )
    p_out.start()

    for copy in a_fwd:
        copy.wait_recv()

    rows = stage.shape[1]
    steps = depth // rows
    width = g_buf.shape[1]
    columns = 512 if width % 512 == 0 else 128

    def write(slot, row):
        return pltpu.make_async_copy(
            stage.at[slot], merged_ref.at[pl.ds(row, rows)], stage_sems.at[slot]
        )

    def merge(i, _):
        slot = lax.rem(i, 2)
        row = pl.multiple_of(i * rows, rows)

        @pl.when(i >= 2)
        def _():
            write(slot, row).wait()

        lhs = a_buf[:, pl.ds(row, rows)].T
        for j in range(width // columns):
            cols = slice(j * columns, (j + 1) * columns)
            stage[slot, :, cols] = dot(lhs, g_buf[:, cols], ((1,), (0,))).astype(BF16)
        write(slot, row).start()
        return 0

    u_both = jnp.concatenate(split(dot(p_high, a_buf[...], ((1,), (1,)))), axis=0)
    term = dot(u_both, g_buf[...], ((1,), (0,)))
    term = (term[:rank] + term[rank:]) * (1.0 / nd)
    q_f32[...] = term
    for j in range(nd):
        q_part[j] = term[j * q_rows : (j + 1) * q_rows].astype(q_part.dtype)
    copies = [
        send(q_part.at[z_peer(d)], q_recv.at[d], qrs_sems.at[d], "dp", z_peer(d))
        for d in range(1, nd)
    ]
    lax.fori_loop(0, steps // 2, merge, 0)
    total = q_f32[pl.ds(pl.multiple_of(z * q_rows, q_rows), q_rows), :]
    for d, copy in zip(range(1, nd), copies):
        copy.wait_recv()
        total = total + q_recv[d].astype(F32)
    q_all[z] = total.astype(q_all.dtype)
    copies = [
        send(q_all.at[z], q_all.at[z], qag_sems.at[d], "dp", z_peer(d)) for d in range(1, nd)
    ]
    lax.fori_loop(steps // 2, steps, merge, 0)
    for copy in copies:
        copy.wait_recv()
    q_out = pltpu.make_async_copy(q_all, qnew_ref, local_sems.at[5])
    q_out.start()
    for copy in pending:
        copy.wait_send()
    for slot in range(2):
        write(slot, 0).wait()
    p_out.wait()
    q_out.wait()


def factors(nt, nd, activations, out_grads, q_t):
    tok, depth = activations.shape[1:]
    tokens, width = out_grads.shape[1:]
    rank = q_t.shape[0]
    nx = nt // 2
    pair = 2 * tok
    pieces = min(4, tok // 16)
    part = depth // nt
    chunk = part // nd
    q_rows = rank // nd
    q_type = BF16 if q_rows % 16 == 0 else F32
    dma = pltpu.SemaphoreType.DMA
    anywhere = pl.BlockSpec(memory_space=pl.ANY)
    return pl.pallas_call(
        functools.partial(factors_kernel, nt, nd),
        out_shape=(
            pltpu.VMEM((depth, width), BF16),
            pltpu.VMEM((2 * rank, depth), BF16),
            pltpu.VMEM((nd, q_rows, width), q_type),
        ),
        in_specs=[anywhere] * 3,
        out_specs=(anywhere, anywhere, anywhere),
        scratch_shapes=[
            pltpu.VMEM((tokens, depth), BF16),
            pltpu.VMEM((tokens, width), BF16),
            pltpu.VMEM((rank, width), BF16),
            pltpu.VMEM((nx, rank, pair), F32),
            pltpu.VMEM((nx, rank, pair), F32),
            pltpu.VMEM((nx, rank, pair), F32),
            pltpu.VMEM((nx, rank, pair), F32),
            pltpu.VMEM((nx, rank, part), F32),
            pltpu.VMEM((nx, rank, part), F32),
            pltpu.VMEM((nd, rank, chunk), F32),
            pltpu.VMEM((nd, rank, chunk), F32),
            pltpu.VMEM((nt, nd, rank, chunk), F32),
            pltpu.VMEM((rank, depth), F32),
            pltpu.VMEM((2 * rank, depth), BF16),
            pltpu.VMEM((rank, width), F32),
            pltpu.VMEM((nd, q_rows, width), q_type),
            pltpu.VMEM((nd, q_rows, width), q_type),
            pltpu.VMEM((nd, q_rows, width), q_type),
            pltpu.VMEM((2, 512, width), BF16),
            dma((6,)),
            dma((2,)),
            dma((2,)),
            dma((nx, 2, pieces)),
            dma((nx, 2, pieces)),
            dma((2,)),
            dma((nx, 2)),
            dma((nx, 2)),
            dma((nd, 2)),
            dma((nd, 2)),
            dma((2, nd)),
            dma((nx, 2, nd)),
            dma((nx, 2, nd)),
            dma((nd, 2)),
            dma((nd, 2)),
        ],
        compiler_params=pltpu.CompilerParams(
            collective_id=0, has_side_effects=True, vmem_limit_bytes=34 * 2**20
        ),
        name="factors",
    )(activations, out_grads, q_t)


def finish_kernel(own, z_ref, merged_ref, pneg_ref, q_ref, wu_ref, qnew_ref, err_ref, lhs, both):
    step = pl.program_id(0)
    width = merged_ref.shape[1]
    rank = q_ref.shape[0]
    lhs[...] = pneg_ref[...].T

    @pl.when(step == 0)
    def _():
        both[0:rank] = q_ref[...].astype(BF16)
        both[rank : 2 * rank] = q_ref[...].astype(BF16)
        qnew_ref[...] = q_ref[...].astype(F32)

    columns = 512 if width % 512 == 0 else 128
    rows = err_ref.shape[1]
    block = lax.rem(step + z_ref[0] * own, pl.num_programs(0))
    here = pl.ds(pl.multiple_of(block * rows, rows), rows)

    def tiles(update):
        for j in range(width // columns):
            cols = slice(j * columns, (j + 1) * columns)
            minus = dot(lhs[...], both[:, cols], ((1,), (0,)))
            err_ref[0, :, cols] = (merged_ref[here, cols].astype(F32) + minus).astype(BF16)
            if update:
                wu_ref[:, cols] = (-minus).astype(BF16)

    pl.when(step < own)(lambda: tiles(True))
    pl.when(step >= own)(lambda: tiles(False))


def finish(nd, merged, p_neg, q_t):
    depth, width = merged.shape
    rank = q_t.shape[0]
    rows = 256
    steps = depth // rows
    own = steps // nd

    def at(i, z):
        return lax.rem(i + z[0] * own, steps)

    z = lax.axis_index("dp").astype(jnp.int32).reshape(1)
    return pl.pallas_call(
        functools.partial(finish_kernel, own),
        out_shape=(
            jax.ShapeDtypeStruct((depth // nd, width), BF16),
            jax.ShapeDtypeStruct((rank, width), F32),
            jax.ShapeDtypeStruct((1, depth, width), BF16),
        ),
        grid_spec=pltpu.PrefetchScalarGridSpec(
            num_scalar_prefetch=1,
            grid=(steps,),
            in_specs=[
                pl.BlockSpec(memory_space=pltpu.VMEM),
                pl.BlockSpec((2 * rank, rows), lambda i, z: (0, at(i, z))),
                pl.BlockSpec((rank, width), lambda i, z: (0, 0)),
            ],
            out_specs=(
                pl.BlockSpec((rows, width), lambda i, z: (jnp.minimum(i, own - 1), 0)),
                pl.BlockSpec((rank, width), lambda i, z: (0, 0)),
                pl.BlockSpec((1, rows, width), lambda i, z: (0, at(i, z), 0)),
            ),
            scratch_shapes=[
                pltpu.VMEM((rows, 2 * rank), BF16),
                pltpu.VMEM((2 * rank, width), BF16),
            ],
        ),
        compiler_params=pltpu.CompilerParams(
            dimension_semantics=("arbitrary",), vmem_limit_bytes=34 * 2**20
        ),
        name="finish",
    )(z, merged, p_neg, q_t)


def per_device(nt, nd, activations, out_grads, q_start):
    merged, p_neg, q_parts = factors(nt, nd, activations, out_grads, q_start.T)
    q_t = q_parts.reshape(q_start.shape[1], out_grads.shape[2])
    merged, p_neg, q_t = (
        pltpu.with_memory_space_constraint(x, pltpu.VMEM) for x in (merged, p_neg, q_t)
    )
    weight_update, q_new, new_error = finish(nd, merged, p_neg, q_t)
    return weight_update, q_new.T, new_error


def solution(mesh):
    return jax.shard_map(
        functools.partial(per_device, mesh.shape["tensor"], mesh.shape["dp"]),
        mesh=mesh,
        in_specs=(
            P(("groups", "dp"), "tensor", None),
            P(("groups", "dp"), None, "tensor"),
            P(("groups", "tensor"), None),
        ),
        out_specs=(
            P(("groups", "dp"), "tensor"),
            P(("groups", "tensor"), None),
            P(("groups", "dp"), None, "tensor"),
        ),
        check_vma=False,
    )
```
